512 devices in a mesh: lat: 16 (over y_hi, z), lon: 32 (over x, y_lo, core).
Axes of the slice: x: 4, y: 8 (y_hi: 2, y_lo: 4; y = y_hi * 4 + y_lo), z: 8, core: 2. Of those that a mesh axis runs over, the one named last changes fastest.
Arguments:
- tokens: bfloat16 [4, 96, 1152, 512], P(None, 'lat', 'lon'), may hold values from -6 to 6
- gain_attn: float32 [512], replicated, may hold values from 0.1 to 1.9
- gain_mlp: float32 [512], replicated, may hold values from 0.1 to 1.9
- w_qkv: bfloat16 [512, 1536], P('lon'), may hold values from -1 to 1
- w_proj: bfloat16 [512, 512], P('lon'), may hold values from -0.25 to 0.25
- w_up: bfloat16 [512, 2048], P('lon'), may hold values from -0.25 to 0.25
- w_down: bfloat16 [2048, 512], P('lon'), may hold values from -0.125 to 0.125
Outputs:
- block_out: bfloat16 [4, 96, 1152, 512], P(None, 'lat', 'lon')
The draws below stay inside these ranges and needn't reach their ends.
All inputs are finite; a program needn't handle non-finite values.
Results may differ from the reference program's by a relative error of at most 0.0055.
Values may be sent and summed in bfloat16 or wider, within the bound.
No kernel may reach another device: no remote copies, remote signals or barrier semaphores. Data moves between devices by JAX's collectives and lax.ppermute only.
A program may use at most 128 MiB of HBM per device.

```python
import jax
import jax.numpy as jnp
from jax import lax

D = 512
HEADS = 8
FF = 2048
LEV = 4
WIN_LEV = 2
WIN_LAT = 6
WIN_LON = 12
NLAT = 96
NLON = 1152


def draw_w_qkv(key, part):
    key = jax.random.fold_in(key, 11)
    base = jax.random.normal(key, (D, 3 * D), jnp.float32)
    full = jnp.clip(base, -4.0, 4.0) / jnp.sqrt(jnp.float32(D))
    return full.astype(jnp.bfloat16)


def block_scale(stream_key, dims, shards, low, top_value):
    factor_of, own = 1.0, jax.random.fold_in(stream_key, 6)
    for dim, blocks in shards:
        heights = jnp.exp(jax.random.uniform(jax.random.fold_in(own, dim), (blocks,), jnp.float32, low / len(shards), top_value / len(shards)))
        factor_of = factor_of * jnp.repeat(heights, dims[dim] // blocks).reshape([-1 if axis == dim else 1 for axis in range(len(dims))])
    return factor_of


def bell_draw(own_key, extent, scale, limit, split=(), held_as=jnp.bfloat16):
    level = block_scale(own_key, extent, split, -0.22, 0.18) if split else 1.0
    drawn = jax.random.normal(own_key, extent, jnp.float32) * scale * level
    return jnp.minimum(jnp.maximum(drawn, -limit), limit).astype(held_as)


def setup_inputs(seed: int = 0) -> dict:
    key_list = jax.random.split(jax.random.key(seed), 8)
    return {
        "tokens": bell_draw(key_list[0], (LEV, NLAT, NLON, D), 1.0, 6.0, ((1, 16), (2, 32))),
        "gain_attn": jnp.clip(1.0 + 0.18 * jax.random.normal(key_list[1], (D,), jnp.float32), 0.1, 1.9),
        "gain_mlp": jnp.clip(1.0 + 0.18 * jax.random.normal(key_list[2], (D,), jnp.float32), 0.1, 1.9),
        "w_qkv": draw_w_qkv(jax.random.fold_in(key_list[7], 71), 0),
        "w_proj": bell_draw(key_list[4], (D, D), D ** -0.5, 0.25, ((0, 32),)),
        "w_up": bell_draw(key_list[5], (D, FF), D ** -0.5, 0.25, ((0, 32),)),
        "w_down": bell_draw(key_list[6], (FF, D), FF ** -0.5, 0.125, ((0, 32),)),
    }


def layer_norm(values, gain):
    values = values.astype(jnp.float32)
    center = values - lax.optimization_barrier(jnp.mean(values, axis=-1, keepdims=True))
    spread = lax.optimization_barrier(jnp.mean(center * center, axis=-1, keepdims=True))
    return center * lax.rsqrt(spread + 1e-05) * gain

def attend(region, lat_labels, gain_attn, full_qkv):
    levels, rows, columns, features = region.shape
    head_size = features // HEADS
    normed = layer_norm(region, gain_attn).astype(jnp.bfloat16)
    projected = jnp.dot(normed.reshape(-1, features), full_qkv, preferred_element_type=jnp.float32).astype(jnp.bfloat16)
    projected = projected.reshape(levels // WIN_LEV, WIN_LEV, rows // WIN_LAT, WIN_LAT, columns // WIN_LON, WIN_LON, 3, HEADS, head_size)
    projected = projected.transpose(0, 2, 4, 6, 7, 1, 3, 5, 8)
    windows = levels // WIN_LEV * (rows // WIN_LAT) * (columns // WIN_LON)
    span = WIN_LEV * WIN_LAT * WIN_LON
    projected = projected.reshape(windows, 3, HEADS, span, head_size)
    query = projected[:, 0].astype(jnp.float32)
    keys = projected[:, 1].astype(jnp.float32)
    values = projected[:, 2].astype(jnp.float32)
    level_pos = jnp.arange(levels)
    level_labels = jnp.where(level_pos < levels - WIN_LEV, 0, jnp.where(level_pos < levels - WIN_LEV // 2, 1, 2))
    labels = level_labels[:, None] * 3 + lat_labels[None, :]
    labels = jnp.broadcast_to(labels[:, :, None], (levels, rows, columns))
    labels = labels.reshape(levels // WIN_LEV, WIN_LEV, rows // WIN_LAT, WIN_LAT, columns // WIN_LON, WIN_LON)
    labels = labels.transpose(0, 2, 4, 1, 3, 5).reshape(windows, span)
    allowed = labels[:, :, None] == labels[:, None, :]
    scores = jnp.einsum('whqd,whkd->whqk', query, keys) * head_size ** (-0.5)
    scores = jnp.where(allowed[:, None], scores, -jnp.inf)
    scores = scores - lax.optimization_barrier(jnp.max(scores, axis=-1, keepdims=True))
    expo = jnp.exp(scores)
    probability = (expo / lax.optimization_barrier(jnp.sum(expo, axis=-1, keepdims=True))).astype(jnp.bfloat16)
    attended = jnp.einsum('whqk,whkd->whqd', probability.astype(jnp.float32), values).astype(jnp.bfloat16)
    attended = attended.reshape(levels // WIN_LEV, rows // WIN_LAT, columns // WIN_LON, HEADS, WIN_LEV, WIN_LAT, WIN_LON, head_size)
    attended = attended.transpose(0, 4, 1, 5, 2, 6, 3, 7)
    return attended.reshape(-1, features)

def finish(residual_in, attended, full_proj, gain_mlp, full_up, full_down):
    residual = residual_in.astype(jnp.float32) + jnp.dot(attended, full_proj, preferred_element_type=jnp.float32)
    normed = layer_norm(residual, gain_mlp).astype(jnp.bfloat16)
    hidden = jax.nn.gelu(jnp.dot(normed, full_up, preferred_element_type=jnp.float32), approximate=False).astype(jnp.bfloat16)
    return (residual + jnp.dot(hidden, full_down, preferred_element_type=jnp.float32)).astype(jnp.bfloat16)

def reference(tokens, gain_attn, gain_mlp, w_qkv, w_proj, w_up, w_down):
    shifts = (WIN_LEV // 2, WIN_LAT // 2, WIN_LON // 2)
    rolled = jnp.roll(tokens, (-shifts[0], -shifts[1], -shifts[2]), axis=(0, 1, 2))
    levels, total_rows, total_columns, features = tokens.shape
    bands = total_rows // WIN_LAT

    def one_band(band):
        block = lax.dynamic_slice_in_dim(rolled, band * WIN_LAT, WIN_LAT, 1)
        position = band * WIN_LAT + jnp.arange(WIN_LAT)
        lat_labels = jnp.where(position < total_rows - WIN_LAT, 0, jnp.where(position < total_rows - WIN_LAT // 2, 1, 2))
        attended = attend(block, lat_labels, gain_attn, w_qkv)
        result = finish(block.reshape(-1, features), attended, w_proj, gain_mlp, w_up, w_down)
        return result.reshape(block.shape)
    done = lax.map(one_band, jnp.arange(bands, dtype=jnp.int32))
    done = done.transpose(1, 0, 2, 3, 4).reshape(tokens.shape)
    return jnp.roll(done, shifts, axis=(0, 1, 2))
```

```python
import functools

import jax
import jax.numpy as jnp
from jax import lax
from jax.experimental import pallas as pl
from jax.experimental.pallas import tpu as pltpu
from jax.sharding import Mesh
from jax.sharding import PartitionSpec as P

BF16 = jnp.bfloat16
F32 = jnp.float32
LEV, ROWS, COLS, D = 4, 6, 36, 512
HALF, RIM = 3, 6
REG = ROWS + 2 * HALF
SLOT = 16
WINS = 4
PAD = 40
FLAT = LEV * ROWS * PAD
FF = 2048
QKV = 3 * D
REST = D + FF + 4 * D
OFFSETS = (0, 3, 1, 2)
VMEM = 56 * 1024 * 1024


def norm(values, gain):
    center = values - jnp.mean(values, axis=-1, keepdims=True)
    spread = jnp.mean(center * center, axis=-1, keepdims=True)
    return center * lax.rsqrt(spread + 1e-05) * gain


def shard_row(pos, mine, outer, inner):
    x, y, core = pos
    owner = core if mine else 1 - core
    first = owner == 0
    a, b = OFFSETS[outer], OFFSETS[inner]
    sx = lax.rem(x + jnp.where(first, a, b), 4)
    sy = lax.rem(y + jnp.where(first, b, a), 4)
    return sx * 8 + sy * 2 + owner


def pieces_of(refs):
    own, other = refs[:4], refs[4:]
    result = [(True, o, i, own[o].at[i]) for o in range(4) for i in range(4)]
    per = 4 // len(other)
    for o in range(4):
        for i in range(4):
            result.append((False, o, i, other[o // per].at[(o % per) * 4 + i]))
    return result


def place_tokens(stage, row, gain, main, west, east, xn_ref, dst):
    stage[row, 64:100, :] = norm(main.astype(F32), gain)
    stage[row, 0:RIM, :] = norm(west.astype(F32), gain)
    stage[row, 54:60, :] = norm(east.astype(F32), gain)
    stage[row, 6:12, :] = stage[row, 64:70, :]
    stage[row, 16:28, :] = stage[row, 70:82, :]
    stage[row, 32:44, :] = stage[row, 82:94, :]
    stage[row, 48:54, :] = stage[row, 94:100, :]
    xn_ref[dst] = stage[row, 0:64, :].reshape(WINS, SLOT, D).astype(BF16)


def attn_kernel(position, n_w, gain_ref, tok_ref, north_ref, south_ref, west_ref, east_ref, *refs):
    w_refs = refs[:n_w]
    out_ref, w_ref, stage, xn_ref, q_ref, kv_ref, nat_ref, sem = refs[n_w:]
    pos, band = position()
    copies = []
    for mine, o, i, src in pieces_of(w_refs):
        at = pl.multiple_of(shard_row(pos, mine, o, i) * 16, 16)
        copies.append(pltpu.make_async_copy(src, w_ref.at[pl.ds(at, 16), :], sem))
    for c in copies:
        c.start()

    gain = gain_ref[...]
    for r in range(REG):
        for s in range(WINS):
            stage[r, 16 * s + 8 : 16 * s + 16, :] = jnp.zeros((8, D), F32)

    def place(lev, _):
        for r in range(REG):
            if r < HALF:
                main = north_ref[lev, r]
            elif r < HALF + ROWS:
                main = tok_ref[lev, r - HALF]
            else:
                main = south_ref[lev, r - HALF - ROWS]
            place_tokens(
                stage, r, gain, main, west_ref[lev, r], east_ref[lev, r], xn_ref, lev * REG + r
            )
        return 0

    lax.fori_loop(0, LEV, place, 0)

    for c in copies:
        c.wait()

    def project(lev, _):
        rows = xn_ref[pl.ds(lev * REG, REG)].reshape(REG * WINS * SLOT, D)
        for part in range(2):
            kv = jnp.dot(
                rows, w_ref[:, D * (part + 1) : D * (part + 2)], preferred_element_type=F32
            ).astype(BF16)
            kv_ref[pl.ds(lev * REG, REG), :, :, D * part : D * (part + 1)] = kv.reshape(
                REG, WINS, SLOT, D
            )
        mine = xn_ref[pl.ds(lev * REG + HALF, ROWS)].reshape(ROWS * WINS * SLOT, D)
        q = jnp.dot(mine, w_ref[:, 0:D], preferred_element_type=F32).astype(BF16)
        q_ref[pl.ds(lev * ROWS, ROWS)] = (q * jnp.asarray(0.125, BF16)).reshape(ROWS, WINS, SLOT, D)
        return 0

    lax.fori_loop(0, LEV, project, 0)

    lane = lax.broadcasted_iota(jnp.int32, (1, 256), 1) // 64

    def window(h, j, levels, half):
        feats = slice(256 * half, 256 * half + 256)
        vals = slice(D + 256 * half, D + 256 * half + 256)
        n_q, n_k = len(levels) * HALF * SLOT, len(levels) * ROWS * SLOT
        q = jnp.concatenate(
            [q_ref[pl.ds(lv * ROWS + HALF * h, HALF), j, :, feats] for lv in levels], axis=0
        ).reshape(n_q, 256)
        k = jnp.concatenate(
            [kv_ref[pl.ds(lv * REG + ROWS * h, ROWS), j, :, feats] for lv in levels], axis=0
        ).reshape(n_k, 256)
        v = jnp.concatenate(
            [kv_ref[pl.ds(lv * REG + ROWS * h, ROWS), j, :, vals] for lv in levels], axis=0
        ).reshape(n_k, 256)
        key = lax.broadcasted_iota(jnp.int32, (1, n_k), 1)
        key_row = lax.rem(key // SLOT, ROWS)
        first_row = jnp.where(jnp.logical_and(h == 0, band == 0), HALF, 0)
        last_row = jnp.where(jnp.logical_and(h == 1, band == 15), HALF, ROWS)
        bias = jnp.where(lax.rem(key, SLOT) >= 2 * RIM, -jnp.inf, 0.0)
        bias = jnp.where(key_row < first_row, -jnp.inf, bias)
        bias = jnp.where(key_row >= last_row, -jnp.inf, bias)
        packed = jnp.concatenate(
            [jnp.where(lane == hh, q, jnp.zeros_like(q)) for hh in range(4)], axis=0
        )
        s = lax.dot_general(packed, k, (((1,), (1,)), ((), ())), preferred_element_type=F32)
        s = s + bias
        p = jnp.exp(s - jnp.max(s, axis=-1, keepdims=True))
        total = jnp.sum(p, axis=-1, keepdims=True)
        o = jnp.dot(p.astype(BF16), v, preferred_element_type=F32)
        o = o * (1.0 / total)
        result = o[0:n_q]
        for hh in range(1, 4):
            result = jnp.where(lane == hh, o[hh * n_q : (hh + 1) * n_q], result)
        return result.reshape(len(levels), HALF, SLOT, 256)

    starts = (0, 6, 18, 30)

    def attend(h, _):
        for j in range(WINS):
            skip, count = (RIM, RIM) if j == 0 else (0, RIM) if j == 3 else (0, 2 * RIM)
            for levels in ((1, 2), (0,), (3,)):
                for half in range(2):
                    got = window(h, j, levels, half)
                    for n, lv in enumerate(levels):
                        for r in range(HALF):
                            row = (lv * ROWS + HALF * h + r) * PAD
                            row = pl.multiple_of(row, 8)
                            block = nat_ref.at[pl.ds(row, PAD), 256 * half : 256 * half + 256]
                            block[starts[j] : starts[j] + count, :] = got[n, r, skip : skip + count]
        return 0

    lax.fori_loop(0, 2, attend, 0)

    for r in range(LEV * ROWS):
        nat_ref[r * PAD + COLS : (r + 1) * PAD, :] = jnp.zeros((PAD - COLS, D), F32)
    out_ref[...] = nat_ref[...].astype(BF16)


def attend_call(position, gain, tokens, north, south, west, east, pieces, interpret=False):
    vmem = pl.BlockSpec(memory_space=pltpu.VMEM)
    anywhere = pl.BlockSpec(memory_space=pl.ANY)
    return pl.pallas_call(
        functools.partial(attn_kernel, position, len(pieces)),
        out_shape=jax.ShapeDtypeStruct((FLAT, D), BF16),
        in_specs=[vmem] * 6 + [anywhere] * len(pieces),
        out_specs=vmem,
        scratch_shapes=[
            pltpu.VMEM((D, QKV), BF16),
            pltpu.VMEM((REG, 104, D), F32),
            pltpu.VMEM((LEV * REG, WINS, SLOT, D), BF16),
            pltpu.VMEM((LEV * ROWS, WINS, SLOT, D), BF16),
            pltpu.VMEM((LEV * REG, WINS, SLOT, 2 * D), BF16),
            pltpu.VMEM((FLAT, D), F32),
            pltpu.SemaphoreType.DMA,
        ],
        compiler_params=pltpu.CompilerParams(vmem_limit_bytes=VMEM),
        interpret=interpret,
        name="attention",
    )(gain, tokens, north, south, west, east, *pieces)


MLP_ROWS = 240


def mlp_kernel(position, n_w, gain_ref, tok_ref, att_ref, *refs):
    w_refs = refs[:n_w]
    out_ref, pu_ref, dn_ref, x_ref, sem = refs[n_w:]
    pos, _ = position()
    copies = []
    for mine, o, i, src in pieces_of(w_refs):
        shard = shard_row(pos, mine, o, i)
        at = pl.multiple_of(shard * 16, 16)
        copies.append(
            pltpu.make_async_copy(src.at[:, 0 : D + FF], pu_ref.at[pl.ds(at, 16), :], sem)
        )
        for n in range(4):
            at = pl.multiple_of(shard * 64 + 16 * n, 16)
            lo = D + FF + D * n
            copies.append(
                pltpu.make_async_copy(src.at[:, lo : lo + D], dn_ref.at[pl.ds(at, 16), :], sem)
            )
    for c in copies:
        c.start()
    for r in range(LEV * ROWS):
        x_ref[r * PAD : r * PAD + COLS, :] = tok_ref[r].astype(F32)
        x_ref[r * PAD + COLS : (r + 1) * PAD, :] = jnp.zeros((PAD - COLS, D), F32)
    for c in copies:
        c.wait()

    gain = gain_ref[...]

    def chunk(n, _):
        rows = pl.ds(pl.multiple_of(n * MLP_ROWS, 16), MLP_ROWS)
        residual = x_ref[rows, :] + jnp.dot(
            att_ref[rows, :], pu_ref[:, 0:D], preferred_element_type=F32
        )
        normed = norm(residual, gain).astype(BF16)
        total = residual
        for f in range(4):
            up = jnp.dot(
                normed, pu_ref[:, D + D * f : D + D * (f + 1)], preferred_element_type=F32
            )
            hidden = (0.5 * up * (1.0 + lax.erf(up * 0.7071067811865476))).astype(BF16)
            total = total + jnp.dot(
                hidden, dn_ref[D * f : D * (f + 1), :], preferred_element_type=F32
            )
        x_ref[rows, :] = total
        return 0

    lax.fori_loop(0, FLAT // MLP_ROWS, chunk, 0)
    for r in range(LEV * ROWS):
        out_ref[r] = x_ref[r * PAD : r * PAD + COLS, :].astype(BF16)


def mlp_call(position, gain, tokens, attended, pieces, interpret=False):
    vmem = pl.BlockSpec(memory_space=pltpu.VMEM)
    anywhere = pl.BlockSpec(memory_space=pl.ANY)
    return pl.pallas_call(
        functools.partial(mlp_kernel, position, len(pieces)),
        out_shape=jax.ShapeDtypeStruct((LEV * ROWS, COLS, D), BF16),
        in_specs=[vmem] * 3 + [anywhere] * len(pieces),
        out_specs=vmem,
        scratch_shapes=[
            pltpu.VMEM((D, D + FF), BF16),
            pltpu.VMEM((FF, D), BF16),
            pltpu.VMEM((FLAT, D), F32),
            pltpu.SemaphoreType.DMA,
        ],
        compiler_params=pltpu.CompilerParams(vmem_limit_bytes=VMEM),
        interpret=interpret,
        name="mlp",
    )(gain, tokens, attended, *pieces)


AXES = ("yh", "z", "x", "yl", "core")
SIZES = (2, 8, 4, 4, 2)


def number(yh, z, x, yl, core):
    return (((yh * 8 + z) * 4 + x) * 4 + yl) * 2 + core


def each_device():
    for yh in range(2):
        for z in range(8):
            for x in range(4):
                for yl in range(4):
                    for core in range(2):
                        yield yh, z, x, yl, core


def ring_pairs(by, first):
    pairs = []
    for yh, z, x, yl, core in each_device():
        if (core == 0) == first:
            y = (yh * 4 + yl + by) % 8
            to = number(y // 4, z, x, y % 4, core)
        else:
            to = number(yh, z, (x + by) % 4, yl, core)
        pairs.append((number(yh, z, x, yl, core), to))
    return pairs


def lat_pairs(by):
    pairs = []
    for yh, z, x, yl, core in each_device():
        band = yh * 8 + z + by
        if 0 <= band < 16:
            pairs.append((number(yh, z, x, yl, core), number(band // 8, band % 8, x, yl, core)))
    return pairs


def lon_pairs(by):
    pairs = []
    for yh, z, x, yl, core in each_device():
        lon = ((x * 4 + yl) * 2 + core + by) % 32
        pairs.append((number(yh, z, x, yl, core), number(yh, z, lon // 8, lon // 2 % 4, lon % 2)))
    return pairs


def core_pairs():
    return [(number(*d), number(*d[:4], 1 - d[4])) for d in each_device()]


def send(value, pairs):
    return lax.ppermute(value, AXES, pairs)


def gather_stage(block, first):
    return [
        block,
        send(block, ring_pairs(1, first)),
        send(block, ring_pairs(-1, first)),
        send(block, ring_pairs(2, first)),
    ]


def position():
    pos = (lax.axis_index("x"), lax.axis_index("yl"), lax.axis_index("core"))
    return pos, lax.axis_index("yh") * 8 + lax.axis_index("z")


def body(tokens, gain_attn, gain_mlp, w_qkv, w_proj, w_up, w_down):
    north = send(tokens[:, ROWS - HALF :], lat_pairs(1))
    south = send(tokens[:, :HALF], lat_pairs(-1))
    shard = jnp.concatenate(
        [w_qkv, w_proj, w_up] + [w_down[16 * n : 16 * n + 16] for n in range(4)], axis=1
    )
    line = jnp.stack(gather_stage(shard, True))
    region = jnp.concatenate([north, tokens, south], axis=1)
    west = send(region[:, :, COLS - RIM :], lon_pairs(1))
    east = send(region[:, :, :RIM], lon_pairs(-1))

    own_a = gather_stage(line[:, :, :QKV], False)
    other_a = send(jnp.concatenate(own_a, axis=0), core_pairs())
    own_b = gather_stage(line[:, :, QKV:], False)
    other_b = [
        send(jnp.concatenate(own_b[:2], axis=0), core_pairs()),
        send(jnp.concatenate(own_b[2:], axis=0), core_pairs()),
    ]
    attended = attend_call(
        position, gain_attn.reshape(1, D), tokens, north, south, west, east, own_a + [other_a]
    )
    done = mlp_call(
        position,
        gain_mlp.reshape(1, D),
        tokens.reshape(LEV * ROWS, COLS, D),
        attended,
        own_b + other_b,
    )
    return done.reshape(LEV, ROWS, COLS, D)


def solution(mesh):
    torus = Mesh(mesh.devices.reshape(SIZES), AXES)
    weight = P(("x", "yl", "core"), None)
    grid = P(None, ("yh", "z"), ("x", "yl", "core"), None)
    return jax.shard_map(
        body,
        mesh=torus,
        in_specs=(grid, P(), P(), weight, weight, weight, weight),
        out_specs=grid,
        check_vma=False,
    )
```

```python
import functools

import jax
import jax.numpy as jnp
from jax import lax
from jax.experimental import pallas as pl
from jax.experimental.pallas import tpu as pltpu
from jax.sharding import Mesh
from jax.sharding import PartitionSpec as P

BF16 = jnp.bfloat16
F32 = jnp.float32
LEV, ROWS, COLS, D = 4, 6, 36, 512
HALF, RIM = 3, 6
REG = ROWS + 2 * HALF
SLOT = 16
WINS = 4
LINE = COLS * LEV
EDGE = RIM * LEV
STRIP = 32
REGION = LINE + 2 * STRIP
DIRECT = 80
WIDE = LINE + 2 * EDGE
SPREAD = WINS * LEV * SLOT
FF = 2048
QKV = 3 * D
REST = D + FF + 4 * D
OFFSETS = (0, 3, 1, 2)
VMEM = 56 * 1024 * 1024


def norm(values, gain):
    center = values - jnp.mean(values, axis=-1, keepdims=True)
    spread = jnp.mean(center * center, axis=-1, keepdims=True)
    return center * lax.rsqrt(spread + 1e-05) * gain


def whole():
    return pl.BlockSpec(memory_space=pltpu.VMEM)


def anywhere():
    return pl.BlockSpec(memory_space=pltpu.HBM)


def pack_kernel(position, gain_ref, tok_ref, qkv_ref, proj_ref, up_ref, down_ref, *outs):
    w_ref, top_ref, low_ref, direct_ref, hop_ref = outs
    w_ref[:, 0:QKV] = qkv_ref[...]
    w_ref[:, QKV : QKV + D] = proj_ref[...]
    w_ref[:, QKV + D : QKV + D + FF] = up_ref[...]
    for n in range(4):
        lo = QKV + D + FF + D * n
        w_ref[:, lo : lo + D] = down_ref[16 * n : 16 * n + 16, :]
    gain = gain_ref[...]
    for r in range(HALF):
        for out_ref, n in ((top_ref, r), (low_ref, r + HALF)):
            line = tok_ref[n].astype(F32).reshape(LINE, D)
            out_ref[r] = norm(line, gain).astype(BF16)
    band = position()[1]

    def middle(ref):
        direct_ref[...] = ref[:, 0:DIRECT, :]
        hop_ref[...] = ref[:, DIRECT:LINE, :]

    @pl.when(band == 7)
    def _():
        middle(low_ref)

    @pl.when(band != 7)
    def _():
        middle(top_ref)


def pack_call(position, gain, tokens, w_qkv, w_proj, w_up, w_down):
    def rows(n):
        return jax.ShapeDtypeStruct((HALF, n, D), BF16)

    return pl.pallas_call(
        functools.partial(pack_kernel, position),
        out_shape=[
            jax.ShapeDtypeStruct((16, QKV + REST), BF16),
            rows(LINE),
            rows(LINE),
            rows(DIRECT),
            rows(LINE - DIRECT),
        ],
        in_specs=[whole()] * 6,
        out_specs=[whole()] * 5,
        compiler_params=pltpu.CompilerParams(vmem_limit_bytes=VMEM),
        name="pack",
    )(gain, tokens, w_qkv, w_proj, w_up, w_down)


def place(pos, mine, other, moves):
    x, y, core = pos
    spans = ((0, 0, 4), (3, 0, 4), (1, 0, 4), (2, 0, 2), (2, 2, 2))

    def copies(own_is_first, move):
        low, count, target, sem = move
        result = []
        for refs, first in ((mine, own_is_first), (other, not own_is_first)):
            for source, (offset, start, size) in zip(refs, spans):
                inner = slice(start, start + size)
                if first:
                    where = (lax.rem(x + offset, 4), inner, 0)
                else:
                    where = (inner, lax.rem(y + offset, 4), 1)
                result.append(
                    pltpu.make_async_copy(source.at[:, :, low : low + count], target(where), sem)
                )
        return result

    def each(move, act):
        for own_is_first in (True, False):

            @pl.when(core == (0 if own_is_first else 1))
            def _(own_is_first=own_is_first):
                for c in copies(own_is_first, move):
                    act(c)

    for move in moves:
        each(move, lambda c: c.start())
    return [lambda move=move: each(move, lambda c: c.wait()) for move in moves]


def edge_kernel(position, top_ref, low_ref, north_ref, south_ref, direct_ref, hop_ref, east_ref, west_ref):
    band = position()[1]
    ends = ((east_ref, slice(LINE - STRIP, LINE), hop_ref, slice(LINE - DIRECT - STRIP, LINE - DIRECT)),
            (west_ref, slice(0, STRIP), direct_ref, slice(0, STRIP)))
    for out_ref, cols, middle_ref, middle_cols in ends:
        out_ref[0:HALF] = north_ref[:, cols, :]
        out_ref[HALF : 2 * HALF] = top_ref[:, cols, :]
        out_ref[2 * HALF : 3 * HALF] = low_ref[:, cols, :]
        out_ref[3 * HALF :] = south_ref[:, cols, :]

        @pl.when(band == 8)
        def _():
            out_ref[0:HALF] = middle_ref[:, middle_cols, :]

        @pl.when(band == 7)
        def _():
            out_ref[3 * HALF :] = middle_ref[:, middle_cols, :]


def edge_call(position, *halo):
    return pl.pallas_call(
        functools.partial(edge_kernel, position),
        out_shape=[jax.ShapeDtypeStruct((REG, STRIP, D), BF16)] * 2,
        in_specs=[whole()] * 6,
        out_specs=[whole()] * 2,
        compiler_params=pltpu.CompilerParams(vmem_limit_bytes=VMEM),
        cost_estimate=pl.CostEstimate(
            flops=10**10, transcendentals=0, bytes_accessed=8 * 1024 * 1024
        ),
        name="edges",
    )(*halo)


def slot_source(index):
    j = index // (LEV * SLOT)
    level = lax.rem(index // SLOT, LEV)
    col = lax.rem(index, SLOT)
    return jnp.where(col < 2 * RIM, (j * 2 * RIM + col) * LEV + level, -1)


CHUNK_ROWS = 3


def block_kernel(position, gain_ref, tok_hbm, *refs):
    top, low, north, south, direct, hop, west, east = refs[:8]
    mine, (near, rest), out_ref = refs[8:13], refs[13:15], refs[15]
    other = [near.at[0:4], near.at[4:8], near.at[8:12], rest.at[0:2], rest.at[2:4]]
    tok_ref, reg_ref, w_ref, pu_ref, dn_ref, q_ref, kv_ref, att_ref = refs[16:24]
    tok_sem, reg_sem, w_sem, pu_sem, dn_sem = refs[24:]
    pos, band = position()
    fetch = pltpu.make_async_copy(tok_hbm, tok_ref, tok_sem)
    main = slice(STRIP, STRIP + LINE)
    first = slice(STRIP, STRIP + DIRECT)
    second = slice(STRIP + DIRECT, STRIP + LINE)

    def into(source, rows, cols):
        return pltpu.make_async_copy(source, reg_ref.at[rows, cols], reg_sem)

    above, below = slice(0, HALF), slice(3 * HALF, REG)
    always = [
        into(top, slice(HALF, 2 * HALF), main),
        into(low, slice(2 * HALF, 3 * HALF), main),
        into(west, slice(0, REG), slice(0, STRIP)),
        into(east, slice(0, REG), slice(STRIP + LINE, REGION)),
    ]
    from_north, from_south = into(north, above, main), into(south, below, main)
    from_8 = [into(direct, above, first), into(hop, above, second)]
    from_7 = [into(direct, below, first), into(hop, below, second)]

    def region(act):
        for c in always:
            act(c)

        @pl.when(band == 8)
        def _():
            for c in from_8:
                act(c)

        @pl.when(band != 8)
        def _():
            act(from_north)

        @pl.when(band == 7)
        def _():
            for c in from_7:
                act(c)

        @pl.when(band != 7)
        def _():
            act(from_south)

    region(lambda c: c.start())
    moves = [
        (0, QKV, lambda where: w_ref.at[where], w_sem),
        (QKV, D + FF, lambda where: pu_ref.at[where], pu_sem),
    ]
    for n in range(4):
        moves.append(
            (QKV + D + FF + D * n, D, lambda where, n=n: dn_ref.at[where + (n,)], dn_sem)
        )
    wait_qkv, *waits = place(pos, mine, other, moves)
    fetch.start()

    source = slot_source(lax.broadcasted_iota(jnp.int32, (SPREAD, REGION), 0))
    token = lax.broadcasted_iota(jnp.int32, (SPREAD, REGION), 1) - (STRIP - EDGE)
    spread = jnp.where(source == token, 1.0, 0.0).astype(BF16)
    region(lambda c: c.wait())
    wait_qkv()
    for r in range(REG):
        rows = jnp.dot(spread, reg_ref[r], preferred_element_type=F32).astype(BF16)
        kv = jnp.dot(
            rows, w_ref[:, :, :, :, D:].reshape(D, 2 * D), preferred_element_type=F32
        ).astype(BF16)
        kv_ref[r] = kv.reshape(WINS, LEV, SLOT, 2 * D)
        if HALF <= r < HALF + ROWS:
            q = jnp.dot(
                rows, w_ref[:, :, :, :, 0:D].reshape(D, D), preferred_element_type=F32
            ).astype(BF16)
            q_ref[r - HALF] = (q * jnp.asarray(0.125, BF16)).reshape(WINS, LEV, SLOT, D)

    lane = lax.broadcasted_iota(jnp.int32, (1, 256), 1) // 64

    def window(h, j, levels, half):
        feats = slice(256 * half, 256 * half + 256)
        vals = slice(D + 256 * half, D + 256 * half + 256)
        n_q, n_k = len(levels) * HALF * SLOT, len(levels) * ROWS * SLOT
        q = jnp.concatenate(
            [q_ref[pl.ds(HALF * h, HALF), j, lv, :, feats] for lv in levels], axis=0
        ).reshape(n_q, 256)
        k = jnp.concatenate(
            [kv_ref[pl.ds(ROWS * h, ROWS), j, lv, :, feats] for lv in levels], axis=0
        ).reshape(n_k, 256)
        v = jnp.concatenate(
            [kv_ref[pl.ds(ROWS * h, ROWS), j, lv, :, vals] for lv in levels], axis=0
        ).reshape(n_k, 256)
        key = lax.broadcasted_iota(jnp.int32, (1, n_k), 1)
        key_row = lax.rem(key // SLOT, ROWS)
        first_row = jnp.where(jnp.logical_and(h == 0, band == 0), HALF, 0)
        last_row = jnp.where(jnp.logical_and(h == 1, band == 15), HALF, ROWS)
        bias = jnp.where(lax.rem(key, SLOT) >= 2 * RIM, -jnp.inf, 0.0)
        bias = jnp.where(key_row < first_row, -jnp.inf, bias)
        bias = jnp.where(key_row >= last_row, -jnp.inf, bias)
        packed = jnp.concatenate(
            [jnp.where(lane == hh, q, jnp.zeros_like(q)) for hh in range(4)], axis=0
        )
        s = lax.dot_general(packed, k, (((1,), (1,)), ((), ())), preferred_element_type=F32)
        s = s + bias
        p = jnp.exp(s - jnp.max(s, axis=-1, keepdims=True))
        total = jnp.sum(p, axis=-1, keepdims=True)
        o = jnp.dot(p.astype(BF16), v, preferred_element_type=F32)
        o = o * (1.0 / total)
        result = o[0:n_q]
        for hh in range(1, 4):
            result = jnp.where(lane == hh, o[hh * n_q : (hh + 1) * n_q], result)
        result = result.astype(BF16).reshape(len(levels), HALF, SLOT, 256)
        for n, lv in enumerate(levels):
            att_ref[pl.ds(HALF * h, HALF), j, lv, :, feats] = result[n]

    def attend(n, _):
        h, j = n // WINS, lax.rem(n, WINS)
        for levels in ((1, 2), (0,), (3,)):
            for half in range(2):
                window(h, j, levels, half)
        return 0

    lax.fori_loop(0, 2 * WINS, attend, 0, unroll=8)

    token = lax.broadcasted_iota(jnp.int32, (LINE, SPREAD), 0) + EDGE
    source = slot_source(lax.broadcasted_iota(jnp.int32, (LINE, SPREAD), 1))
    gather = jnp.where(source == token, 1.0, 0.0).astype(BF16)
    waits[0]()
    fetch.wait()
    gain = gain_ref[...]

    def widen(n):
        rows = slice(n * CHUNK_ROWS, (n + 1) * CHUNK_ROWS)
        attended = jnp.concatenate(
            [
                jnp.dot(
                    gather, att_ref[r].reshape(SPREAD, D), preferred_element_type=F32
                ).astype(BF16)
                for r in range(n * CHUNK_ROWS, (n + 1) * CHUNK_ROWS)
            ],
            axis=0,
        )
        residual = tok_ref[rows].astype(F32).reshape(CHUNK_ROWS * LINE, D) + jnp.dot(
            attended, pu_ref[:, :, :, :, 0:D].reshape(D, D), preferred_element_type=F32
        )
        return residual, norm(residual, gain).astype(BF16)

    def hide(normed, f):
        up = jnp.dot(
            normed,
            pu_ref[:, :, :, :, D + D * f : D + D * (f + 1)].reshape(D, D),
            preferred_element_type=F32,
        )
        return (0.5 * up * (1.0 + lax.erf(up * 0.7071067811865476))).astype(BF16)

    for n in range(ROWS // CHUNK_ROWS):
        total, normed = widen(n)
        for f in range(4):
            hidden = hide(normed, f)
            if n == 0 and f == 0:
                for wait in waits[1:]:
                    wait()
            total = total + jnp.dot(
                hidden, dn_ref[f].reshape(D, D), preferred_element_type=F32
            )
        rows = slice(n * CHUNK_ROWS, (n + 1) * CHUNK_ROWS)
        out_ref[rows] = total.reshape(CHUNK_ROWS, COLS, LEV, D).astype(BF16)


def block_call(position, gain, tokens, halo, mine, other):
    return pl.pallas_call(
        functools.partial(block_kernel, position),
        out_shape=jax.ShapeDtypeStruct((ROWS, COLS, LEV, D), BF16),
        in_specs=[whole()] + [anywhere()] * 16,
        out_specs=whole(),
        scratch_shapes=[
            pltpu.VMEM((ROWS, COLS, LEV, D), BF16),
            pltpu.VMEM((REG, REGION, D), BF16),
            pltpu.VMEM((4, 4, 2, 16, QKV), BF16),
            pltpu.VMEM((4, 4, 2, 16, D + FF), BF16),
            pltpu.VMEM((4, 4, 2, 4, 16, D), BF16),
            pltpu.VMEM((ROWS, WINS, LEV, SLOT, D), BF16),
            pltpu.VMEM((REG, WINS, LEV, SLOT, 2 * D), BF16),
            pltpu.VMEM((ROWS, WINS, LEV, SLOT, D), BF16),
        ]
        + [pltpu.SemaphoreType.DMA] * 5,
        compiler_params=pltpu.CompilerParams(vmem_limit_bytes=VMEM),
        name="block",
    )(gain, tokens, *halo, *mine, *other)


AXES = ("yh", "z", "x", "yl", "core")
SIZES = (2, 8, 4, 4, 2)


def number(yh, z, x, yl, core):
    return (((yh * 8 + z) * 4 + x) * 4 + yl) * 2 + core


def each_device():
    for yh in range(2):
        for z in range(8):
            for x in range(4):
                for yl in range(4):
                    for core in range(2):
                        yield yh, z, x, yl, core


def ring_pairs(by, first):
    pairs = []
    for yh, z, x, yl, core in each_device():
        if (core == 0) == first:
            y = yh * 4 + yl
            y = (y + (-by if by == 2 and y % 2 else by)) % 8
            to = number(y // 4, z, x, y % 4, core)
        else:
            to = number(yh, z, (x + by) % 4, yl, core)
        pairs.append((number(yh, z, x, yl, core), to))
    return pairs


def lat_pairs(by):
    pairs = []
    for yh, z, x, yl, core in each_device():
        if 0 <= z + by < 8:
            pairs.append((number(yh, z, x, yl, core), number(yh, z + by, x, yl, core)))
    return pairs


def middle_pairs():
    pairs = []
    for yh, z, x, yl, core in each_device():
        if (yh, z) in ((0, 7), (1, 0)):
            pairs.append((number(yh, z, x, yl, core), number(1 - yh, 7 - z, x, yl, core)))
    return pairs


def hop_pairs():
    pairs = []
    for yh, z, x, yl, core in each_device():
        if (yh, z) in ((0, 7), (1, 0)):
            pairs.append((number(yh, z, x, yl, core), number(yh, 7 - z, x, yl, core)))
    return pairs


def onward_pairs():
    pairs = []
    for yh, z, x, yl, core in each_device():
        if (yh, z) in ((0, 0), (1, 7)):
            pairs.append((number(yh, z, x, yl, core), number(1 - yh, z, x, yl, core)))
    return pairs


def lon_pairs(by):
    pairs = []
    for yh, z, x, yl, core in each_device():
        lon = ((x * 4 + yl) * 2 + core + by) % 32
        pairs.append((number(yh, z, x, yl, core), number(yh, z, lon // 8, lon // 2 % 4, lon % 2)))
    return pairs


def core_pairs():
    return [(number(*d), number(*d[:4], 1 - d[4])) for d in each_device()]


def send(value, pairs):
    return lax.ppermute(value, AXES, pairs)


def gather_stage(block, first):
    return [
        block,
        send(block, ring_pairs(1, first)),
        send(block, ring_pairs(-1, first)),
        send(block, ring_pairs(2, first)),
    ]


def position():
    pos = (lax.axis_index("x"), lax.axis_index("yl"), lax.axis_index("core"))
    return pos, lax.axis_index("yh") * 8 + lax.axis_index("z")


def body(tokens, gain_attn, gain_mlp, w_qkv, w_proj, w_up, w_down):
    (x, y, core), band = position()
    tok = tokens.transpose(1, 2, 0, 3)
    packed, top, low, direct, hop = pack_call(
        position, gain_attn.reshape(1, D), tok, w_qkv, w_proj, w_up, w_down
    )
    direct = send(direct, middle_pairs())
    hop = send(send(hop, hop_pairs()), onward_pairs())
    north = send(low, lat_pairs(1))
    south = send(top, lat_pairs(-1))

    mine, behind, ahead, far = gather_stage(packed, True)
    me = jnp.where(core == 0, y, x)
    ordered = []
    for n in range(4):
        ahead_by = lax.rem(n + 4 - me, 4)
        block = jnp.where(ahead_by == 3, behind, mine)
        block = jnp.where(ahead_by == 1, ahead, block)
        ordered.append(jnp.where(ahead_by == 2, far, block))
    line = lax.optimization_barrier(jnp.stack(ordered))
    behind = send(line, ring_pairs(1, False))
    ahead = send(line, ring_pairs(-1, False))
    to_east, to_west = edge_call(position, top, low, north, south, direct, hop)
    behind, ahead, to_east, to_west = lax.optimization_barrier((behind, ahead, to_east, to_west))
    far = [send(behind[:2], ring_pairs(1, False)), send(ahead[2:], ring_pairs(-1, False))]
    own = [line, behind, ahead, *far]
    west = send(to_east, lon_pairs(1))
    east = send(to_west, lon_pairs(-1))
    far, west, east = lax.optimization_barrier((far, west, east))
    near = send(jnp.concatenate([line, behind, ahead], axis=0), core_pairs())
    rest = send(jnp.concatenate(far, axis=0), core_pairs())

    halo = [top, low, north, south, direct, hop, west, east]
    done = block_call(position, gain_mlp.reshape(1, D), tok, halo, own, [near, rest])
    return done.transpose(2, 0, 1, 3)


def solution(mesh):
    torus = Mesh(mesh.devices.reshape(SIZES), AXES)
    weight = P(("x", "yl", "core"), None)
    grid = P(None, ("yh", "z"), ("x", "yl", "core"), None)
    return jax.shard_map(
        body,
        mesh=torus,
        in_specs=(grid, P(), P(), weight, weight, weight, weight),
        out_specs=grid,
        check_vma=False,
    )
```

```python
import functools

import jax
import jax.numpy as jnp
from jax import lax
from jax.experimental import pallas as pl
from jax.experimental.pallas import tpu as pltpu
from jax.sharding import Mesh
from jax.sharding import PartitionSpec as P

BF16 = jnp.bfloat16
F32 = jnp.float32
LEV, ROWS, COLS, D = 4, 6, 36, 512
HALF, RIM = 3, 6
REG = ROWS + 2 * HALF
SLOT = 16
WINS = 4
LINE = COLS * LEV
EDGE = RIM * LEV
STRIP = 32
REGION = LINE + 2 * STRIP
DIRECT = 80
WIDE = LINE + 2 * EDGE
SPREAD = WINS * LEV * SLOT
FF = 2048
QKV = 3 * D
REST = D + FF + 4 * D
OFFSETS = (0, 3, 1, 2)
VMEM = 56 * 1024 * 1024


def norm(values, gain):
    center = values - jnp.mean(values, axis=-1, keepdims=True)
    spread = jnp.mean(center * center, axis=-1, keepdims=True)
    return center * lax.rsqrt(spread + 1e-05) * gain


def whole():
    return pl.BlockSpec(memory_space=pltpu.VMEM)


def anywhere():
    return pl.BlockSpec(memory_space=pltpu.HBM)


def pack_kernel(position, gain_ref, tok_ref, qkv_ref, proj_ref, up_ref, down_ref, *outs):
    w_ref, top_ref, low_ref, direct_ref, hop_ref = outs
    w_ref[:, 0:QKV] = qkv_ref[...]
    w_ref[:, QKV : QKV + D] = proj_ref[...]
    w_ref[:, QKV + D : QKV + D + FF] = up_ref[...]
    for n in range(4):
        lo = QKV + D + FF + D * n
        w_ref[:, lo : lo + D] = down_ref[16 * n : 16 * n + 16, :]
    gain = gain_ref[...]
    for r in range(HALF):
        for out_ref, n in ((top_ref, r), (low_ref, r + HALF)):
            line = tok_ref[n].astype(F32).reshape(LINE, D)
            out_ref[r] = norm(line, gain).astype(BF16)
    band = position()[1]

    def middle(ref):
        direct_ref[...] = ref[:, 0:DIRECT, :]
        hop_ref[...] = ref[:, DIRECT:LINE, :]

    @pl.when(band == 7)
    def _():
        middle(low_ref)

    @pl.when(band != 7)
    def _():
        middle(top_ref)


def pack_call(position, gain, tokens, w_qkv, w_proj, w_up, w_down):
    def rows(n):
        return jax.ShapeDtypeStruct((HALF, n, D), BF16)

    return pl.pallas_call(
        functools.partial(pack_kernel, position),
        out_shape=[
            jax.ShapeDtypeStruct((16, QKV + REST), BF16),
            rows(LINE),
            rows(LINE),
            rows(DIRECT),
            rows(LINE - DIRECT),
        ],
        in_specs=[whole()] * 6,
        out_specs=[whole()] * 5,
        compiler_params=pltpu.CompilerParams(vmem_limit_bytes=VMEM),
        name="pack",
    )(gain, tokens, w_qkv, w_proj, w_up, w_down)


def place(pos, mine, other, moves):
    x, y, core = pos
    spans = ((0, 0, 4), (3, 0, 4), (1, 0, 4), (2, 0, 2), (2, 2, 2))

    def copies(own_is_first, move):
        low, count, target, sem = move
        result = []
        for refs, first in ((mine, own_is_first), (other, not own_is_first)):
            for source, (offset, start, size) in zip(refs, spans):
                inner = slice(start, start + size)
                if first:
                    where = (lax.rem(x + offset, 4), inner, 0)
                else:
                    where = (inner, lax.rem(y + offset, 4), 1)
                result.append(
                    pltpu.make_async_copy(source.at[:, :, low : low + count], target(where), sem)
                )
        return result

    def each(move, act):
        for own_is_first in (True, False):

            @pl.when(core == (0 if own_is_first else 1))
            def _(own_is_first=own_is_first):
                for c in copies(own_is_first, move):
                    act(c)

    for move in moves:
        each(move, lambda c: c.start())
    return [lambda move=move: each(move, lambda c: c.wait()) for move in moves]


def edge_kernel(position, top_ref, low_ref, north_ref, south_ref, direct_ref, hop_ref, east_ref, west_ref):
    band = position()[1]
    ends = ((east_ref, slice(LINE - STRIP, LINE), hop_ref, slice(LINE - DIRECT - STRIP, LINE - DIRECT)),
            (west_ref, slice(0, STRIP), direct_ref, slice(0, STRIP)))
    for out_ref, cols, middle_ref, middle_cols in ends:
        out_ref[0:HALF] = north_ref[:, cols, :]
        out_ref[HALF : 2 * HALF] = top_ref[:, cols, :]
        out_ref[2 * HALF : 3 * HALF] = low_ref[:, cols, :]
        out_ref[3 * HALF :] = south_ref[:, cols, :]

        @pl.when(band == 8)
        def _():
            out_ref[0:HALF] = middle_ref[:, middle_cols, :]

        @pl.when(band == 7)
        def _():
            out_ref[3 * HALF :] = middle_ref[:, middle_cols, :]


def edge_call(position, *halo):
    return pl.pallas_call(
        functools.partial(edge_kernel, position),
        out_shape=[jax.ShapeDtypeStruct((REG, STRIP, D), BF16)] * 2,
        in_specs=[whole()] * 6,
        out_specs=[whole()] * 2,
        compiler_params=pltpu.CompilerParams(vmem_limit_bytes=VMEM),
        cost_estimate=pl.CostEstimate(
            flops=10**10, transcendentals=0, bytes_accessed=8 * 1024 * 1024
        ),
        name="edges",
    )(*halo)


def slot_source(index):
    j = index // (LEV * SLOT)
    level = lax.rem(index // SLOT, LEV)
    col = lax.rem(index, SLOT)
    return jnp.where(col < 2 * RIM, (j * 2 * RIM + col) * LEV + level, -1)


CHUNK_ROWS = 3


def block_kernel(position, gain_ref, tok_hbm, *refs):
    top, low, north, south, direct, hop, west, east = refs[:8]
    mine, other, out_ref = refs[8:13], refs[13:18], refs[18]
    tok_ref, reg_ref, w_ref, pu_ref, dn_ref, q_ref, kv_ref, att_ref = refs[19:27]
    tok_sem, reg_sem, w_sem, pu_sem, dn_sem = refs[27:]
    pos, band = position()
    fetch = pltpu.make_async_copy(tok_hbm, tok_ref, tok_sem)
    main = slice(STRIP, STRIP + LINE)
    near = slice(STRIP, STRIP + DIRECT)
    rest = slice(STRIP + DIRECT, STRIP + LINE)

    def into(source, rows, cols):
        return pltpu.make_async_copy(source, reg_ref.at[rows, cols], reg_sem)

    above, below = slice(0, HALF), slice(3 * HALF, REG)
    always = [
        into(top, slice(HALF, 2 * HALF), main),
        into(low, slice(2 * HALF, 3 * HALF), main),
        into(west, slice(0, REG), slice(0, STRIP)),
        into(east, slice(0, REG), slice(STRIP + LINE, REGION)),
    ]
    from_north, from_south = into(north, above, main), into(south, below, main)
    from_8 = [into(direct, above, near), into(hop, above, rest)]
    from_7 = [into(direct, below, near), into(hop, below, rest)]

    def region(act):
        for c in always:
            act(c)

        @pl.when(band == 8)
        def _():
            for c in from_8:
                act(c)

        @pl.when(band != 8)
        def _():
            act(from_north)

        @pl.when(band == 7)
        def _():
            for c in from_7:
                act(c)

        @pl.when(band != 7)
        def _():
            act(from_south)

    region(lambda c: c.start())
    moves = [
        (0, QKV, lambda where: w_ref.at[where], w_sem),
        (QKV, D + FF, lambda where: pu_ref.at[where], pu_sem),
    ]
    for n in range(4):
        moves.append(
            (QKV + D + FF + D * n, D, lambda where, n=n: dn_ref.at[where + (n,)], dn_sem)
        )
    wait_qkv, *waits = place(pos, mine, other, moves)
    fetch.start()

    source = slot_source(lax.broadcasted_iota(jnp.int32, (SPREAD, REGION), 0))
    token = lax.broadcasted_iota(jnp.int32, (SPREAD, REGION), 1) - (STRIP - EDGE)
    spread = jnp.where(source == token, 1.0, 0.0).astype(BF16)
    region(lambda c: c.wait())
    wait_qkv()
    for r in range(REG):
        rows = jnp.dot(spread, reg_ref[r], preferred_element_type=F32).astype(BF16)
        kv = jnp.dot(
            rows, w_ref[:, :, :, :, D:].reshape(D, 2 * D), preferred_element_type=F32
        ).astype(BF16)
        kv_ref[r] = kv.reshape(WINS, LEV, SLOT, 2 * D)
        if HALF <= r < HALF + ROWS:
            q = jnp.dot(
                rows, w_ref[:, :, :, :, 0:D].reshape(D, D), preferred_element_type=F32
            ).astype(BF16)
            q_ref[r - HALF] = (q * jnp.asarray(0.125, BF16)).reshape(WINS, LEV, SLOT, D)

    lane = lax.broadcasted_iota(jnp.int32, (1, 256), 1) // 64

    def window(h, j, levels, half):
        feats = slice(256 * half, 256 * half + 256)
        vals = slice(D + 256 * half, D + 256 * half + 256)
        n_q, n_k = len(levels) * HALF * SLOT, len(levels) * ROWS * SLOT
        q = jnp.concatenate(
            [q_ref[pl.ds(HALF * h, HALF), j, lv, :, feats] for lv in levels], axis=0
        ).reshape(n_q, 256)
        k = jnp.concatenate(
            [kv_ref[pl.ds(ROWS * h, ROWS), j, lv, :, feats] for lv in levels], axis=0
        ).reshape(n_k, 256)
        v = jnp.concatenate(
            [kv_ref[pl.ds(ROWS * h, ROWS), j, lv, :, vals] for lv in levels], axis=0
        ).reshape(n_k, 256)
        key = lax.broadcasted_iota(jnp.int32, (1, n_k), 1)
        key_row = lax.rem(key // SLOT, ROWS)
        first_row = jnp.where(jnp.logical_and(h == 0, band == 0), HALF, 0)
        last_row = jnp.where(jnp.logical_and(h == 1, band == 15), HALF, ROWS)
        bias = jnp.where(lax.rem(key, SLOT) >= 2 * RIM, -jnp.inf, 0.0)
        bias = jnp.where(key_row < first_row, -jnp.inf, bias)
        bias = jnp.where(key_row >= last_row, -jnp.inf, bias)
        packed = jnp.concatenate(
            [jnp.where(lane == hh, q, jnp.zeros_like(q)) for hh in range(4)], axis=0
        )
        s = lax.dot_general(packed, k, (((1,), (1,)), ((), ())), preferred_element_type=F32)
        s = s + bias
        p = jnp.exp(s - jnp.max(s, axis=-1, keepdims=True))
        total = jnp.sum(p, axis=-1, keepdims=True)
        o = jnp.dot(p.astype(BF16), v, preferred_element_type=F32)
        o = o * (1.0 / total)
        result = o[0:n_q]
        for hh in range(1, 4):
            result = jnp.where(lane == hh, o[hh * n_q : (hh + 1) * n_q], result)
        result = result.astype(BF16).reshape(len(levels), HALF, SLOT, 256)
        for n, lv in enumerate(levels):
            att_ref[pl.ds(HALF * h, HALF), j, lv, :, feats] = result[n]

    def attend(n, _):
        h, j = n // WINS, lax.rem(n, WINS)
        for levels in ((1, 2), (0,), (3,)):
            for half in range(2):
                window(h, j, levels, half)
        return 0

    lax.fori_loop(0, 2 * WINS, attend, 0, unroll=8)

    token = lax.broadcasted_iota(jnp.int32, (LINE, SPREAD), 0) + EDGE
    source = slot_source(lax.broadcasted_iota(jnp.int32, (LINE, SPREAD), 1))
    gather = jnp.where(source == token, 1.0, 0.0).astype(BF16)
    waits[0]()
    fetch.wait()
    gain = gain_ref[...]

    def widen(n):
        rows = slice(n * CHUNK_ROWS, (n + 1) * CHUNK_ROWS)
        attended = jnp.concatenate(
            [
                jnp.dot(
                    gather, att_ref[r].reshape(SPREAD, D), preferred_element_type=F32
                ).astype(BF16)
                for r in range(n * CHUNK_ROWS, (n + 1) * CHUNK_ROWS)
            ],
            axis=0,
        )
        residual = tok_ref[rows].astype(F32).reshape(CHUNK_ROWS * LINE, D) + jnp.dot(
            attended, pu_ref[:, :, :, :, 0:D].reshape(D, D), preferred_element_type=F32
        )
        return residual, norm(residual, gain).astype(BF16)

    def hide(normed, f):
        up = jnp.dot(
            normed,
            pu_ref[:, :, :, :, D + D * f : D + D * (f + 1)].reshape(D, D),
            preferred_element_type=F32,
        )
        return (0.5 * up * (1.0 + lax.erf(up * 0.7071067811865476))).astype(BF16)

    for n in range(ROWS // CHUNK_ROWS):
        total, normed = widen(n)
        for f in range(4):
            hidden = hide(normed, f)
            if n == 0 and f == 0:
                for wait in waits[1:]:
                    wait()
            total = total + jnp.dot(
                hidden, dn_ref[f].reshape(D, D), preferred_element_type=F32
            )
        rows = slice(n * CHUNK_ROWS, (n + 1) * CHUNK_ROWS)
        out_ref[rows] = total.reshape(CHUNK_ROWS, COLS, LEV, D).astype(BF16)


def block_call(position, gain, tokens, halo, mine, other):
    return pl.pallas_call(
        functools.partial(block_kernel, position),
        out_shape=jax.ShapeDtypeStruct((ROWS, COLS, LEV, D), BF16),
        in_specs=[whole()] + [anywhere()] * 19,
        out_specs=whole(),
        scratch_shapes=[
            pltpu.VMEM((ROWS, COLS, LEV, D), BF16),
            pltpu.VMEM((REG, REGION, D), BF16),
            pltpu.VMEM((4, 4, 2, 16, QKV), BF16),
            pltpu.VMEM((4, 4, 2, 16, D + FF), BF16),
            pltpu.VMEM((4, 4, 2, 4, 16, D), BF16),
            pltpu.VMEM((ROWS, WINS, LEV, SLOT, D), BF16),
            pltpu.VMEM((REG, WINS, LEV, SLOT, 2 * D), BF16),
            pltpu.VMEM((ROWS, WINS, LEV, SLOT, D), BF16),
        ]
        + [pltpu.SemaphoreType.DMA] * 5,
        compiler_params=pltpu.CompilerParams(vmem_limit_bytes=VMEM),
        name="block",
    )(gain, tokens, *halo, *mine, *other)


AXES = ("yh", "z", "x", "yl", "core")
SIZES = (2, 8, 4, 4, 2)


def number(yh, z, x, yl, core):
    return (((yh * 8 + z) * 4 + x) * 4 + yl) * 2 + core


def each_device():
    for yh in range(2):
        for z in range(8):
            for x in range(4):
                for yl in range(4):
                    for core in range(2):
                        yield yh, z, x, yl, core


def ring_pairs(by, first):
    pairs = []
    for yh, z, x, yl, core in each_device():
        if (core == 0) == first:
            y = yh * 4 + yl
            y = (y + (-by if by == 2 and y % 2 else by)) % 8
            to = number(y // 4, z, x, y % 4, core)
        else:
            to = number(yh, z, (x + by) % 4, yl, core)
        pairs.append((number(yh, z, x, yl, core), to))
    return pairs


def lat_pairs(by):
    pairs = []
    for yh, z, x, yl, core in each_device():
        if 0 <= z + by < 8:
            pairs.append((number(yh, z, x, yl, core), number(yh, z + by, x, yl, core)))
    return pairs


def middle_pairs():
    pairs = []
    for yh, z, x, yl, core in each_device():
        if (yh, z) in ((0, 7), (1, 0)):
            pairs.append((number(yh, z, x, yl, core), number(1 - yh, 7 - z, x, yl, core)))
    return pairs


def hop_pairs():
    pairs = []
    for yh, z, x, yl, core in each_device():
        if (yh, z) in ((0, 7), (1, 0)):
            pairs.append((number(yh, z, x, yl, core), number(yh, 7 - z, x, yl, core)))
    return pairs


def onward_pairs():
    pairs = []
    for yh, z, x, yl, core in each_device():
        if (yh, z) in ((0, 0), (1, 7)):
            pairs.append((number(yh, z, x, yl, core), number(1 - yh, z, x, yl, core)))
    return pairs


def lon_pairs(by):
    pairs = []
    for yh, z, x, yl, core in each_device():
        lon = ((x * 4 + yl) * 2 + core + by) % 32
        pairs.append((number(yh, z, x, yl, core), number(yh, z, lon // 8, lon // 2 % 4, lon % 2)))
    return pairs


def core_pairs():
    return [(number(*d), number(*d[:4], 1 - d[4])) for d in each_device()]


def send(value, pairs):
    return lax.ppermute(value, AXES, pairs)


def gather_stage(block, first):
    return [
        block,
        send(block, ring_pairs(1, first)),
        send(block, ring_pairs(-1, first)),
        send(block, ring_pairs(2, first)),
    ]


def position():
    pos = (lax.axis_index("x"), lax.axis_index("yl"), lax.axis_index("core"))
    return pos, lax.axis_index("yh") * 8 + lax.axis_index("z")


def body(tokens, gain_attn, gain_mlp, w_qkv, w_proj, w_up, w_down):
    (x, y, core), band = position()
    tok = tokens.transpose(1, 2, 0, 3)
    packed, top, low, direct, hop = pack_call(
        position, gain_attn.reshape(1, D), tok, w_qkv, w_proj, w_up, w_down
    )
    direct = send(direct, middle_pairs())
    hop = send(send(hop, hop_pairs()), onward_pairs())
    north = send(low, lat_pairs(1))
    south = send(top, lat_pairs(-1))

    mine, behind, ahead, far = gather_stage(packed, True)
    me = jnp.where(core == 0, y, x)
    ordered = []
    for n in range(4):
        ahead_by = lax.rem(n + 4 - me, 4)
        block = jnp.where(ahead_by == 3, behind, mine)
        block = jnp.where(ahead_by == 1, ahead, block)
        ordered.append(jnp.where(ahead_by == 2, far, block))
    line = jnp.stack(ordered)
    behind = send(line, ring_pairs(1, False))
    ahead = send(line, ring_pairs(-1, False))
    far = [send(behind[:2], ring_pairs(1, False)), send(ahead[2:], ring_pairs(-1, False))]
    own = [line, behind, ahead, *far]
    other = [send(piece, core_pairs()) for piece in own]

    to_east, to_west = edge_call(position, top, low, north, south, direct, hop)
    west = send(to_east, lon_pairs(1))
    east = send(to_west, lon_pairs(-1))
    halo = [top, low, north, south, direct, hop, west, east]
    done = block_call(position, gain_mlp.reshape(1, D), tok, halo, own, other)
    return done.transpose(2, 0, 1, 3)


def solution(mesh):
    torus = Mesh(mesh.devices.reshape(SIZES), AXES)
    weight = P(("x", "yl", "core"), None)
    grid = P(None, ("yh", "z"), ("x", "yl", "core"), None)
    return jax.shard_map(
        body,
        mesh=torus,
        in_specs=(grid, P(), P(), weight, weight, weight, weight),
        out_specs=grid,
        check_vma=False,
    )
```

```python
import functools

import jax
import jax.numpy as jnp
from jax import lax
from jax.experimental import pallas as pl
from jax.experimental.pallas import tpu as pltpu
from jax.sharding import Mesh
from jax.sharding import PartitionSpec as P

BF16 = jnp.bfloat16
F32 = jnp.float32
LEV, ROWS, COLS, D = 4, 6, 36, 512
HALF, RIM = 3, 6
REG = ROWS + 2 * HALF
SLOT = 16
WINS = 4
LINE = COLS * LEV
EDGE = RIM * LEV
STRIP = 32
REGION = LINE + 2 * STRIP
DIRECT = 64
WIDE = LINE + 2 * EDGE
SPREAD = WINS * LEV * SLOT
FF = 2048
QKV = 3 * D
REST = D + FF + 4 * D
OFFSETS = (0, 3, 1, 2)
VMEM = 56 * 1024 * 1024


def norm(values, gain):
    center = values - jnp.mean(values, axis=-1, keepdims=True)
    spread = jnp.mean(center * center, axis=-1, keepdims=True)
    return center * lax.rsqrt(spread + 1e-05) * gain


def whole():
    return pl.BlockSpec(memory_space=pltpu.VMEM)


def anywhere():
    return pl.BlockSpec(memory_space=pltpu.HBM)


def pack_kernel(position, gain_ref, tok_ref, qkv_ref, proj_ref, up_ref, down_ref, *outs):
    w_ref, top_ref, low_ref, direct_ref, hop_ref = outs
    w_ref[:, 0:QKV] = qkv_ref[...]
    w_ref[:, QKV : QKV + D] = proj_ref[...]
    w_ref[:, QKV + D : QKV + D + FF] = up_ref[...]
    for n in range(4):
        lo = QKV + D + FF + D * n
        w_ref[:, lo : lo + D] = down_ref[16 * n : 16 * n + 16, :]
    gain = gain_ref[...]
    for r in range(HALF):
        for out_ref, n in ((top_ref, r), (low_ref, r + HALF)):
            line = tok_ref[n].astype(F32).reshape(LINE, D)
            out_ref[r] = norm(line, gain).astype(BF16)
    band = position()[1]

    def middle(ref):
        direct_ref[...] = ref[:, 0:DIRECT, :]
        hop_ref[...] = ref[:, DIRECT:LINE, :]

    @pl.when(band == 7)
    def _():
        middle(low_ref)

    @pl.when(band != 7)
    def _():
        middle(top_ref)


def pack_call(position, gain, tokens, w_qkv, w_proj, w_up, w_down):
    def rows(n):
        return jax.ShapeDtypeStruct((HALF, n, D), BF16)

    return pl.pallas_call(
        functools.partial(pack_kernel, position),
        out_shape=[
            jax.ShapeDtypeStruct((16, QKV + REST), BF16),
            rows(LINE),
            rows(LINE),
            rows(DIRECT),
            rows(LINE - DIRECT),
        ],
        in_specs=[whole()] * 6,
        out_specs=[whole()] * 5,
        compiler_params=pltpu.CompilerParams(vmem_limit_bytes=VMEM),
        name="pack",
    )(gain, tokens, w_qkv, w_proj, w_up, w_down)


def place(pos, mine, other, moves):
    x, y, core = pos
    spans = ((0, 0, 4), (3, 0, 4), (1, 0, 4), (2, 0, 2), (2, 2, 2))

    def copies(own_is_first, move):
        low, count, target, sem = move
        result = []
        for refs, first in ((mine, own_is_first), (other, not own_is_first)):
            for source, (offset, start, size) in zip(refs, spans):
                inner = slice(start, start + size)
                if first:
                    where = (lax.rem(x + offset, 4), inner, 0)
                else:
                    where = (inner, lax.rem(y + offset, 4), 1)
                result.append(
                    pltpu.make_async_copy(source.at[:, :, low : low + count], target(where), sem)
                )
        return result

    def each(move, act):
        for own_is_first in (True, False):

            @pl.when(core == (0 if own_is_first else 1))
            def _(own_is_first=own_is_first):
                for c in copies(own_is_first, move):
                    act(c)

    for move in moves:
        each(move, lambda c: c.start())
    return [lambda move=move: each(move, lambda c: c.wait()) for move in moves]


def edge_kernel(position, top_ref, low_ref, north_ref, south_ref, direct_ref, hop_ref, east_ref, west_ref):
    band = position()[1]
    ends = ((east_ref, slice(LINE - STRIP, LINE), hop_ref, slice(LINE - DIRECT - STRIP, LINE - DIRECT)),
            (west_ref, slice(0, STRIP), direct_ref, slice(0, STRIP)))
    for out_ref, cols, middle_ref, middle_cols in ends:
        out_ref[0:HALF] = north_ref[:, cols, :]
        out_ref[HALF : 2 * HALF] = top_ref[:, cols, :]
        out_ref[2 * HALF : 3 * HALF] = low_ref[:, cols, :]
        out_ref[3 * HALF :] = south_ref[:, cols, :]

        @pl.when(band == 8)
        def _():
            out_ref[0:HALF] = middle_ref[:, middle_cols, :]

        @pl.when(band == 7)
        def _():
            out_ref[3 * HALF :] = middle_ref[:, middle_cols, :]


def edge_call(position, *halo):
    return pl.pallas_call(
        functools.partial(edge_kernel, position),
        out_shape=[jax.ShapeDtypeStruct((REG, STRIP, D), BF16)] * 2,
        in_specs=[whole()] * 6,
        out_specs=[whole()] * 2,
        compiler_params=pltpu.CompilerParams(vmem_limit_bytes=VMEM),
        cost_estimate=pl.CostEstimate(
            flops=10**10, transcendentals=0, bytes_accessed=8 * 1024 * 1024
        ),
        name="edges",
    )(*halo)


def slot_source(index):
    j = index // (LEV * SLOT)
    level = lax.rem(index // SLOT, LEV)
    col = lax.rem(index, SLOT)
    return jnp.where(col < 2 * RIM, (j * 2 * RIM + col) * LEV + level, -1)


CHUNK_ROWS = 3


def block_kernel(position, gain_ref, tok_hbm, *refs):
    top, low, north, south, direct, hop, west, east = refs[:8]
    mine, other, out_ref = refs[8:13], refs[13:18], refs[18]
    tok_ref, reg_ref, w_ref, pu_ref, dn_ref, q_ref, kv_ref, att_ref = refs[19:27]
    tok_sem, reg_sem, w_sem, pu_sem, dn_sem = refs[27:]
    pos, band = position()
    fetch = pltpu.make_async_copy(tok_hbm, tok_ref, tok_sem)
    main = slice(STRIP, STRIP + LINE)
    near = slice(STRIP, STRIP + DIRECT)
    rest = slice(STRIP + DIRECT, STRIP + LINE)

    def into(source, rows, cols):
        return pltpu.make_async_copy(source, reg_ref.at[rows, cols], reg_sem)

    above, below = slice(0, HALF), slice(3 * HALF, REG)
    always = [
        into(top, slice(HALF, 2 * HALF), main),
        into(low, slice(2 * HALF, 3 * HALF), main),
        into(west, slice(0, REG), slice(0, STRIP)),
        into(east, slice(0, REG), slice(STRIP + LINE, REGION)),
    ]
    from_north, from_south = into(north, above, main), into(south, below, main)
    from_8 = [into(direct, above, near), into(hop, above, rest)]
    from_7 = [into(direct, below, near), into(hop, below, rest)]

    def region(act):
        for c in always:
            act(c)

        @pl.when(band == 8)
        def _():
            for c in from_8:
                act(c)

        @pl.when(band != 8)
        def _():
            act(from_north)

        @pl.when(band == 7)
        def _():
            for c in from_7:
                act(c)

        @pl.when(band != 7)
        def _():
            act(from_south)

    region(lambda c: c.start())
    moves = [
        (0, QKV, lambda where: w_ref.at[where], w_sem),
        (QKV, D + FF, lambda where: pu_ref.at[where], pu_sem),
    ]
    for n in range(4):
        moves.append(
            (QKV + D + FF + D * n, D, lambda where, n=n: dn_ref.at[where + (n,)], dn_sem)
        )
    wait_qkv, *waits = place(pos, mine, other, moves)
    fetch.start()

    source = slot_source(lax.broadcasted_iota(jnp.int32, (SPREAD, REGION), 0))
    token = lax.broadcasted_iota(jnp.int32, (SPREAD, REGION), 1) - (STRIP - EDGE)
    spread = jnp.where(source == token, 1.0, 0.0).astype(BF16)
    region(lambda c: c.wait())
    wait_qkv()
    for r in range(REG):
        rows = jnp.dot(spread, reg_ref[r], preferred_element_type=F32).astype(BF16)
        kv = jnp.dot(
            rows, w_ref[:, :, :, :, D:].reshape(D, 2 * D), preferred_element_type=F32
        ).astype(BF16)
        kv_ref[r] = kv.reshape(WINS, LEV, SLOT, 2 * D)
        if HALF <= r < HALF + ROWS:
            q = jnp.dot(
                rows, w_ref[:, :, :, :, 0:D].reshape(D, D), preferred_element_type=F32
            ).astype(BF16)
            q_ref[r - HALF] = (q * jnp.asarray(0.125, BF16)).reshape(WINS, LEV, SLOT, D)

    lane = lax.broadcasted_iota(jnp.int32, (1, 256), 1) // 64

    def window(h, j, levels, half):
        feats = slice(256 * half, 256 * half + 256)
        vals = slice(D + 256 * half, D + 256 * half + 256)
        n_q, n_k = len(levels) * HALF * SLOT, len(levels) * ROWS * SLOT
        q = jnp.concatenate(
            [q_ref[pl.ds(HALF * h, HALF), j, lv, :, feats] for lv in levels], axis=0
        ).reshape(n_q, 256)
        k = jnp.concatenate(
            [kv_ref[pl.ds(ROWS * h, ROWS), j, lv, :, feats] for lv in levels], axis=0
        ).reshape(n_k, 256)
        v = jnp.concatenate(
            [kv_ref[pl.ds(ROWS * h, ROWS), j, lv, :, vals] for lv in levels], axis=0
        ).reshape(n_k, 256)
        key = lax.broadcasted_iota(jnp.int32, (1, n_k), 1)
        key_row = lax.rem(key // SLOT, ROWS)
        first_row = jnp.where(jnp.logical_and(h == 0, band == 0), HALF, 0)
        last_row = jnp.where(jnp.logical_and(h == 1, band == 15), HALF, ROWS)
        bias = jnp.where(lax.rem(key, SLOT) >= 2 * RIM, -jnp.inf, 0.0)
        bias = jnp.where(key_row < first_row, -jnp.inf, bias)
        bias = jnp.where(key_row >= last_row, -jnp.inf, bias)
        packed = jnp.concatenate(
            [jnp.where(lane == hh, q, jnp.zeros_like(q)) for hh in range(4)], axis=0
        )
        s = lax.dot_general(packed, k, (((1,), (1,)), ((), ())), preferred_element_type=F32)
        s = s + bias
        p = jnp.exp(s - jnp.max(s, axis=-1, keepdims=True))
        total = jnp.sum(p, axis=-1, keepdims=True)
        o = jnp.dot(p.astype(BF16), v, preferred_element_type=F32)
        o = o * (1.0 / total)
        result = o[0:n_q]
        for hh in range(1, 4):
            result = jnp.where(lane == hh, o[hh * n_q : (hh + 1) * n_q], result)
        result = result.astype(BF16).reshape(len(levels), HALF, SLOT, 256)
        for n, lv in enumerate(levels):
            att_ref[pl.ds(HALF * h, HALF), j, lv, :, feats] = result[n]

    def attend(n, _):
        h, j = n // WINS, lax.rem(n, WINS)
        for levels in ((1, 2), (0,), (3,)):
            for half in range(2):
                window(h, j, levels, half)
        return 0

    lax.fori_loop(0, 2 * WINS, attend, 0, unroll=8)

    token = lax.broadcasted_iota(jnp.int32, (LINE, SPREAD), 0) + EDGE
    source = slot_source(lax.broadcasted_iota(jnp.int32, (LINE, SPREAD), 1))
    gather = jnp.where(source == token, 1.0, 0.0).astype(BF16)
    waits[0]()
    fetch.wait()
    gain = gain_ref[...]

    def widen(n):
        rows = slice(n * CHUNK_ROWS, (n + 1) * CHUNK_ROWS)
        attended = jnp.concatenate(
            [
                jnp.dot(
                    gather, att_ref[r].reshape(SPREAD, D), preferred_element_type=F32
                ).astype(BF16)
                for r in range(n * CHUNK_ROWS, (n + 1) * CHUNK_ROWS)
            ],
            axis=0,
        )
        residual = tok_ref[rows].astype(F32).reshape(CHUNK_ROWS * LINE, D) + jnp.dot(
            attended, pu_ref[:, :, :, :, 0:D].reshape(D, D), preferred_element_type=F32
        )
        return residual, norm(residual, gain).astype(BF16)

    def hide(normed, f):
        up = jnp.dot(
            normed,
            pu_ref[:, :, :, :, D + D * f : D + D * (f + 1)].reshape(D, D),
            preferred_element_type=F32,
        )
        return (0.5 * up * (1.0 + lax.erf(up * 0.7071067811865476))).astype(BF16)

    for n in range(ROWS // CHUNK_ROWS):
        total, normed = widen(n)
        for f in range(4):
            hidden = hide(normed, f)
            if n == 0 and f == 0:
                for wait in waits[1:]:
                    wait()
            total = total + jnp.dot(
                hidden, dn_ref[f].reshape(D, D), preferred_element_type=F32
            )
        rows = slice(n * CHUNK_ROWS, (n + 1) * CHUNK_ROWS)
        out_ref[rows] = total.reshape(CHUNK_ROWS, COLS, LEV, D).astype(BF16)


def block_call(position, gain, tokens, halo, mine, other):
    return pl.pallas_call(
        functools.partial(block_kernel, position),
        out_shape=jax.ShapeDtypeStruct((ROWS, COLS, LEV, D), BF16),
        in_specs=[whole()] + [anywhere()] * 19,
        out_specs=whole(),
        scratch_shapes=[
            pltpu.VMEM((ROWS, COLS, LEV, D), BF16),
            pltpu.VMEM((REG, REGION, D), BF16),
            pltpu.VMEM((4, 4, 2, 16, QKV), BF16),
            pltpu.VMEM((4, 4, 2, 16, D + FF), BF16),
            pltpu.VMEM((4, 4, 2, 4, 16, D), BF16),
            pltpu.VMEM((ROWS, WINS, LEV, SLOT, D), BF16),
            pltpu.VMEM((REG, WINS, LEV, SLOT, 2 * D), BF16),
            pltpu.VMEM((ROWS, WINS, LEV, SLOT, D), BF16),
        ]
        + [pltpu.SemaphoreType.DMA] * 5,
        compiler_params=pltpu.CompilerParams(vmem_limit_bytes=VMEM),
        name="block",
    )(gain, tokens, *halo, *mine, *other)


AXES = ("yh", "z", "x", "yl", "core")
SIZES = (2, 8, 4, 4, 2)


def number(yh, z, x, yl, core):
    return (((yh * 8 + z) * 4 + x) * 4 + yl) * 2 + core


def each_device():
    for yh in range(2):
        for z in range(8):
            for x in range(4):
                for yl in range(4):
                    for core in range(2):
                        yield yh, z, x, yl, core


def ring_pairs(by, first):
    pairs = []
    for yh, z, x, yl, core in each_device():
        if (core == 0) == first:
            y = yh * 4 + yl
            y = (y + (-by if by == 2 and y % 2 else by)) % 8
            to = number(y // 4, z, x, y % 4, core)
        else:
            to = number(yh, z, (x + by) % 4, yl, core)
        pairs.append((number(yh, z, x, yl, core), to))
    return pairs


def lat_pairs(by):
    pairs = []
    for yh, z, x, yl, core in each_device():
        if 0 <= z + by < 8:
            pairs.append((number(yh, z, x, yl, core), number(yh, z + by, x, yl, core)))
    return pairs


def middle_pairs():
    pairs = []
    for yh, z, x, yl, core in each_device():
        if (yh, z) in ((0, 7), (1, 0)):
            pairs.append((number(yh, z, x, yl, core), number(1 - yh, 7 - z, x, yl, core)))
    return pairs


def hop_pairs():
    pairs = []
    for yh, z, x, yl, core in each_device():
        if (yh, z) in ((0, 7), (1, 0)):
            pairs.append((number(yh, z, x, yl, core), number(yh, 7 - z, x, yl, core)))
    return pairs


def onward_pairs():
    pairs = []
    for yh, z, x, yl, core in each_device():
        if (yh, z) in ((0, 0), (1, 7)):
            pairs.append((number(yh, z, x, yl, core), number(1 - yh, z, x, yl, core)))
    return pairs


def lon_pairs(by):
    pairs = []
    for yh, z, x, yl, core in each_device():
        lon = ((x * 4 + yl) * 2 + core + by) % 32
        pairs.append((number(yh, z, x, yl, core), number(yh, z, lon // 8, lon // 2 % 4, lon % 2)))
    return pairs


def core_pairs():
    return [(number(*d), number(*d[:4], 1 - d[4])) for d in each_device()]


def send(value, pairs):
    return lax.ppermute(value, AXES, pairs)


def gather_stage(block, first):
    return [
        block,
        send(block, ring_pairs(1, first)),
        send(block, ring_pairs(-1, first)),
        send(block, ring_pairs(2, first)),
    ]


def position():
    pos = (lax.axis_index("x"), lax.axis_index("yl"), lax.axis_index("core"))
    return pos, lax.axis_index("yh") * 8 + lax.axis_index("z")


def body(tokens, gain_attn, gain_mlp, w_qkv, w_proj, w_up, w_down):
    (x, y, core), band = position()
    tok = tokens.transpose(1, 2, 0, 3)
    packed, top, low, direct, hop = pack_call(
        position, gain_attn.reshape(1, D), tok, w_qkv, w_proj, w_up, w_down
    )
    direct = send(direct, middle_pairs())
    hop = send(send(hop, hop_pairs()), onward_pairs())
    north = send(low, lat_pairs(1))
    south = send(top, lat_pairs(-1))

    mine, behind, ahead, far = gather_stage(packed, True)
    me = jnp.where(core == 0, y, x)
    ordered = []
    for n in range(4):
        ahead_by = lax.rem(n + 4 - me, 4)
        block = jnp.where(ahead_by == 3, behind, mine)
        block = jnp.where(ahead_by == 1, ahead, block)
        ordered.append(jnp.where(ahead_by == 2, far, block))
    line = jnp.stack(ordered)
    behind = send(line, ring_pairs(1, False))
    ahead = send(line, ring_pairs(-1, False))
    far = [send(behind[:2], ring_pairs(1, False)), send(ahead[2:], ring_pairs(-1, False))]
    own = [line, behind, ahead, *far]
    other = [send(piece, core_pairs()) for piece in own]

    to_east, to_west = edge_call(position, top, low, north, south, direct, hop)
    west = send(to_east, lon_pairs(1))
    east = send(to_west, lon_pairs(-1))
    halo = [top, low, north, south, direct, hop, west, east]
    done = block_call(position, gain_mlp.reshape(1, D), tok, halo, own, other)
    return done.transpose(2, 0, 1, 3)


def solution(mesh):
    torus = Mesh(mesh.devices.reshape(SIZES), AXES)
    weight = P(("x", "yl", "core"), None)
    grid = P(None, ("yh", "z"), ("x", "yl", "core"), None)
    return jax.shard_map(
        body,
        mesh=torus,
        in_specs=(grid, P(), P(), weight, weight, weight, weight),
        out_specs=grid,
        check_vma=False,
    )
```
